1024 devices in a mesh: row: 32 (over z, x_hi), col: 32 (over x_lo, y, core).
Axes of the slice: x: 8 (x_hi: 4, x_lo: 2; x = x_hi * 2 + x_lo), y: 8, z: 8, core: 2. Of those that a mesh axis runs over, the one named last changes fastest.
Arguments:
- features: bfloat16 [131072, 128], P(('row', 'col')), may hold values from -6 to 6
- weight: bfloat16 [128, 256], replicated, may hold values from -0.5 to 0.5
- tile_vals: bfloat16 [32, 32, 48, 128, 128], P('row', 'col'), may hold values from -0.125 to 0.125
- tile_rows: int32 [32, 32, 48], P('row', 'col'), may hold values from 0 to 31
- tile_cols: int32 [32, 32, 48], P('row', 'col'), may hold values from 0 to 31
- tile_counts: int32 [32, 32], P('row', 'col'), may hold values from 6 to 48, as said below
- cotangent: bfloat16 [131072, 256], P(('row', 'col')), may hold values from -6 to 6
Outputs:
- hidden: bfloat16 [131072, 256], P(('row', 'col'))
- grad_x: bfloat16 [131072, 128], P(('row', 'col'))
- grad_w: float32 [128, 256], replicated
The draws below stay inside these ranges and needn't reach their ends.
Inputs may be any that keep to these rules, and one draw needn't show every extreme that they name: `tile_counts`: slots from this number on are ignored; some partition uses all 48 slots. `tile_rows`: a block pair may occur in several slots of a partition; their tiles add.
All inputs are finite; a program needn't handle non-finite values.
Results may differ from the reference program's by a relative error of at most 0.025.
Values may be sent and summed in bfloat16 or wider, within the bound.
No kernel may reach another device: no remote copies, remote signals or barrier semaphores. Data moves between devices by JAX's collectives and lax.ppermute only.
A program may use at most 32 MiB of HBM per device.

```python
import jax
import jax.numpy as jnp
from jax import lax

F_IN = 128
HID = 256
BLOCK = 128
V_DEV = 128
TILES = 48
ROW_PARTS = 32
COL_PARTS = 32
NV = 131072
RB = 32
CB = 32
N_COL = 32


def draw_tile_counts(key, part):
    key = jax.random.fold_in(key, 11)
    key_base, key_pick = jax.random.split(key)
    partitions = ROW_PARTS * COL_PARTS
    baseline = jax.random.randint(key_base, (partitions,), TILES // 8, TILES // 2 + 1)
    chosen = jax.random.randint(key_pick, (), 0, partitions)
    places = jnp.arange(partitions)
    counts = jnp.where(places == chosen, TILES, baseline)
    return counts.reshape(ROW_PARTS, COL_PARTS).astype(jnp.int32)


def set_ends(entries, rng, least, largest):
    longest = entries.shape.index(max(entries.shape))
    spots = []
    for shift in (0, 1):
        where = [jax.random.randint(jax.random.fold_in(rng, axis), (), 0, length) for axis, length in enumerate(entries.shape)]
        where[longest] = (where[longest] + shift) % entries.shape[longest]
        spots.append(tuple(where))
    return entries.at[spots[0]].set(least).at[spots[1]].set(largest)


def block_levels(stream_key, shape, cuts, least, largest):
    gain = 1.0
    for position, blocks in cuts:
        draws = jax.random.uniform(jax.random.fold_in(jax.random.fold_in(stream_key, 6), position), (blocks,), jnp.float32, least / len(cuts), largest / len(cuts))
        gain = gain * jnp.repeat(jnp.exp(draws), shape[position] // blocks).reshape((-1,) + (1,) * (len(shape) - 1 - position))
    return gain


def normal_values(key, shape, spread, limit, cuts=(), kind=jnp.bfloat16):
    result = jax.random.normal(key, shape, jnp.float32) * spread
    if len(cuts) > 0:
        result = block_levels(key, shape, cuts, -0.22, 0.18) * result
    return jnp.clip(result, min=-limit, max=limit).astype(kind)


def setup_inputs(seed: int = 0) -> dict:
    keys = jax.random.split(jax.random.key(seed), 8)
    features = normal_values(keys[0], (NV, F_IN), 1.0, 6.0, ((0, 1024),))
    weight = normal_values(keys[1], (F_IN, HID), F_IN ** -0.5, 0.5)
    tile_vals = normal_values(keys[2], (ROW_PARTS, COL_PARTS, TILES, BLOCK, BLOCK), (BLOCK * TILES * N_COL // (3 * RB)) ** -0.5, 0.125, ((0, 32), (1, 32)))
    tile_rows = set_ends(jax.random.randint(keys[3], (ROW_PARTS, COL_PARTS, TILES), 0, RB), jax.random.fold_in(keys[3], 1), 0, RB - 1).astype(jnp.int32)
    tile_cols = set_ends(jax.random.randint(keys[4], (ROW_PARTS, COL_PARTS, TILES), 0, CB), jax.random.fold_in(keys[4], 1), 0, CB - 1).astype(jnp.int32)
    tile_counts = draw_tile_counts(jax.random.fold_in(keys[7], 71), 0)
    cotangent = normal_values(keys[6], (NV, HID), 1.0, 6.0, ((0, 1024),))
    return dict(features=features, weight=weight, tile_vals=tile_vals, tile_rows=tile_rows, tile_cols=tile_cols, tile_counts=tile_counts, cotangent=cotangent)


def tile_sums(tile_set, rows_out, rows_in, tile_count, source, n_out, flip):
    width = source.shape[-1]
    source_blocks = source.astype(jnp.float32).reshape(-1, BLOCK, width)

    def visit(summed, item):
        tile, out_id, in_id, slot = item
        picked = lax.dynamic_index_in_dim(source_blocks, in_id, 0, keepdims=False)
        matrix = tile.astype(jnp.float32)
        if flip:
            matrix = matrix.T
        active = (slot < tile_count).astype(jnp.float32)
        product = jnp.dot(matrix, picked, precision=lax.Precision.HIGHEST) * active
        current = lax.dynamic_index_in_dim(summed, out_id, 0, keepdims=False)
        summed = lax.dynamic_update_index_in_dim(summed, current + product, out_id, 0)
        return summed, None

    initial = jnp.zeros((n_out, BLOCK, width), jnp.float32)
    slots = jnp.arange(TILES, dtype=jnp.int32)
    summed, _ = lax.scan(visit, initial, (tile_set, rows_out, rows_in, slots))
    return summed.reshape(n_out * BLOCK, width)


def rounded(values):
    return lax.optimization_barrier(values.astype(jnp.bfloat16)).astype(jnp.float32)


def reference(features, weight, tile_vals, tile_rows, tile_cols, tile_counts, cotangent):
    grid_feat = features.reshape(ROW_PARTS, COL_PARTS, V_DEV, F_IN)

    def forward_row(row_index):
        def over_col(running, col_index):
            stripe = lax.dynamic_index_in_dim(grid_feat, col_index, 1, keepdims=False)
            stripe = stripe.reshape(ROW_PARTS * V_DEV, F_IN)
            term = tile_sums(tile_vals[row_index, col_index], tile_rows[row_index, col_index],
                             tile_cols[row_index, col_index], tile_counts[row_index, col_index],
                             stripe, RB, False)
            return running + rounded(term), None

        start = jnp.zeros((RB * BLOCK, F_IN), jnp.float32)
        running, _ = lax.scan(over_col, start, jnp.arange(COL_PARTS, dtype=jnp.int32))
        return running

    aggregated = lax.map(forward_row, jnp.arange(ROW_PARTS, dtype=jnp.int32)).reshape(NV, F_IN)
    aggregated = aggregated.astype(jnp.bfloat16)
    preact = jnp.dot(aggregated, weight, preferred_element_type=jnp.float32)
    negative = jnp.expm1(jnp.minimum(preact, 0.0))
    hidden = jnp.where(preact > 0, preact, negative).astype(jnp.bfloat16)
    slope = jnp.where(preact > 0, 1.0, negative + 1.0)
    upstream = (cotangent.astype(jnp.float32) * slope).astype(jnp.bfloat16)
    grad_w = jnp.dot(aggregated.T, upstream, preferred_element_type=jnp.float32)
    back_input = jnp.dot(upstream, weight.T, preferred_element_type=jnp.float32).astype(jnp.bfloat16)
    back_rows = back_input.reshape(ROW_PARTS, COL_PARTS * V_DEV, F_IN)

    def backward_col(col_index):
        def over_row(running, row_index):
            stripe = lax.dynamic_index_in_dim(back_rows, row_index, 0, keepdims=False)
            term = tile_sums(tile_vals[row_index, col_index], tile_cols[row_index, col_index],
                             tile_rows[row_index, col_index], tile_counts[row_index, col_index],
                             stripe, CB, True)
            return running + rounded(term), None

        start = jnp.zeros((CB * BLOCK, F_IN), jnp.float32)
        running, _ = lax.scan(over_row, start, jnp.arange(ROW_PARTS, dtype=jnp.int32))
        return running

    by_column = lax.map(backward_col, jnp.arange(COL_PARTS, dtype=jnp.int32))
    grad_x = by_column.reshape(COL_PARTS, ROW_PARTS, V_DEV, F_IN).transpose(1, 0, 2, 3)
    grad_x = grad_x.reshape(NV, F_IN).astype(jnp.bfloat16)
    return hidden, grad_x, grad_w
```

```python
import functools

import jax
import jax.numpy as jnp
from jax import lax
from jax.experimental import pallas as pl
from jax.experimental.pallas import tpu as pltpu
from jax.sharding import Mesh, PartitionSpec as P

ROW = ("z", "x_hi")
PLANE = ("x_lo", "y")
CORE = "core"
COL = PLANE + (CORE,)
UNROLL = 4
VMEM_LIMIT = 32 * 1024 * 1024

SMEM_SPEC = pl.BlockSpec(memory_space=pltpu.SMEM)
VMEM_SPEC = pl.BlockSpec(memory_space=pltpu.VMEM)


def place(block, core):
    return ((block & 1) ^ core) * 16 + (block >> 1)


def add_tiles(count, slots, out_place, product, acc):
    spare = acc.shape[0] - 1

    def group(index, carry):
        first = index * UNROLL
        products = [product(first + j) for j in range(UNROLL)]
        for j in range(UNROLL):
            slot = first + j
            target = jnp.where(slot < count, out_place(slot), spare)
            acc[target] += products[j]
        return carry

    lax.fori_loop(0, (count + UNROLL - 1) // UNROLL, group, 0)


def forward_kernel(count_ref, rows_ref, cols_ref, tiles_ref, stripe_ref, keep_ref, send_ref, acc):
    core = lax.axis_index(CORE)
    acc[...] = jnp.zeros_like(acc)

    def product(k):
        return jnp.dot(tiles_ref[k], stripe_ref[cols_ref[0, k]], preferred_element_type=jnp.float32)

    add_tiles(count_ref[0, 0], tiles_ref.shape[0], lambda k: place(rows_ref[0, k], core), product, acc)
    half = keep_ref.shape[0]
    keep_ref[...] = acc[:half].astype(keep_ref.dtype)
    send_ref[...] = acc[half : 2 * half].astype(send_ref.dtype)


def dense_kernel(terms_ref, weight_ref, cot_ref, hidden_ref, payload_ref):
    groups, owned, _ = terms_ref.shape
    total = terms_ref[0].astype(jnp.float32)
    for i in range(1, groups):
        total += terms_ref[i].astype(jnp.float32)
    aggregated = total.astype(jnp.bfloat16)
    weight = weight_ref[...]
    preact = jnp.dot(aggregated, weight, preferred_element_type=jnp.float32)
    capped = jnp.minimum(preact, 0.0)
    grown = jnp.exp(capped)
    negative = grown - 1.0
    hidden_ref[...] = jnp.where(preact > 0, preact, negative).astype(jnp.bfloat16)
    slope = jnp.where(preact > 0, 1.0, grown)
    upstream = (cot_ref[...].astype(jnp.float32) * slope).astype(jnp.bfloat16)
    grad = lax.dot_general(
        aggregated, upstream, (((0,), (0,)), ((), ())), preferred_element_type=jnp.float32
    )
    back = lax.dot_general(
        weight, upstream, (((1,), (1,)), ((), ())), preferred_element_type=jnp.float32
    ).astype(jnp.bfloat16)
    step = grad.shape[0] // groups
    for i in range(groups):
        piece = grad[i * step : (i + 1) * step]
        packed = jnp.concatenate([piece[:, :128], piece[:, 128:]], axis=0)
        payload_ref[i, :owned] = back
        payload_ref[i, owned:] = packed.astype(jnp.bfloat16)


def backward_kernel(count_ref, rows_ref, cols_ref, tiles_ref, own_ref, other_ref, out_ref, acc, stripe):
    core = lax.axis_index(CORE)
    half = own_ref.shape[0]
    owned = stripe.shape[1]
    stripe[:half] = own_ref[:, :owned]
    stripe[half:] = other_ref[:, :owned]
    acc[...] = jnp.zeros_like(acc)

    def product(k):
        return jnp.dot(stripe[place(rows_ref[0, k], core)], tiles_ref[k], preferred_element_type=jnp.float32)

    add_tiles(count_ref[0, 0], tiles_ref.shape[0], lambda k: cols_ref[0, k], product, acc)
    grad = own_ref[0, owned:].astype(jnp.float32) + other_ref[0, owned:].astype(jnp.float32)
    for i in range(1, half):
        grad += own_ref[i, owned:].astype(jnp.float32) + other_ref[i, owned:].astype(jnp.float32)
    grad = grad.astype(out_ref.dtype)
    for i in range(out_ref.shape[0]):
        out_ref[i, :owned] = acc[i].astype(out_ref.dtype)
        out_ref[i, owned:] = grad


def final_kernel(terms_ref, grad_x_ref, piece_ref):
    groups, rows, owned = terms_ref.shape
    total = terms_ref[0].astype(jnp.float32)
    for i in range(1, groups):
        total += terms_ref[i].astype(jnp.float32)
    grad_x_ref[...] = total[:owned].T.astype(grad_x_ref.dtype)
    step = (rows - owned) // 2
    piece = jnp.concatenate([total[owned : owned + step], total[owned + step :]], axis=1)
    for i in range(piece_ref.shape[0]):
        piece_ref[i] = piece


def call(kernel, name, outs, in_specs, scratch=()):
    return pl.pallas_call(
        kernel,
        name=name,
        out_shape=outs,
        in_specs=in_specs,
        out_specs=jax.tree.map(lambda _: VMEM_SPEC, outs),
        scratch_shapes=list(scratch),
        compiler_params=pltpu.CompilerParams(vmem_limit_bytes=VMEM_LIMIT),
    )


def shards(features, weight, tile_vals, tile_rows, tile_cols, tile_counts, cotangent):
    bf16, f32 = jnp.bfloat16, jnp.float32
    shape = jax.ShapeDtypeStruct
    tiles = tile_vals[0, 0]
    rows, cols = tile_rows[0], tile_cols[0]
    owned, width = features.shape
    hid = weight.shape[1]
    n_row, n_plane = lax.axis_size(ROW), lax.axis_size(PLANE)
    extra = 2 * width // n_plane
    swap = [(0, 1), (1, 0)]
    slot_specs = [SMEM_SPEC, SMEM_SPEC, SMEM_SPEC, VMEM_SPEC]

    spread = jnp.broadcast_to(features[None], (n_row, owned, width))
    stripe = lax.all_to_all(spread, ROW, 0, 0)
    block = shape((n_plane, owned, width), bf16)
    keep, send = call(
        forward_kernel, "forward_tiles", (block, block), slot_specs + [VMEM_SPEC],
        [pltpu.VMEM((2 * n_plane + 1, owned, width), f32)],
    )(tile_counts, rows, cols, tiles, stripe)
    terms = (keep.astype(f32) + lax.ppermute(send, CORE, swap).astype(f32)).astype(bf16)
    terms = lax.all_to_all(terms, PLANE, 0, 0)
    hidden, payload = call(
        dense_kernel, "dense", (shape((owned, hid), bf16), shape((n_plane, owned + extra, width), bf16)),
        [VMEM_SPEC] * 3,
    )(terms, weight, cotangent)
    own = lax.all_to_all(payload, PLANE, 0, 0)
    other = lax.ppermute(own, CORE, swap)
    back = call(
        backward_kernel, "backward_tiles", shape((n_row, width + extra, owned), bf16),
        slot_specs + [VMEM_SPEC] * 2,
        [pltpu.VMEM((n_row + 1, width, owned), f32), pltpu.VMEM((2 * n_plane, width, owned), bf16)],
    )(tile_counts, rows, cols, tiles, own, other)
    back = lax.all_to_all(back, ROW, 0, 0)
    grad_x, piece = call(
        final_kernel, "final", (shape((owned, width), bf16), shape((n_plane, width // n_plane, hid), f32)),
        [VMEM_SPEC],
    )(back)
    grad_w = lax.all_to_all(piece, PLANE, 0, 0).reshape(width, hid)
    return hidden, grad_x, grad_w


def solution(mesh):
    fine = Mesh(mesh.devices.reshape(8, 4, 2, 8, 2), ROW + COL)
    placed = (
        P(ROW + COL, None),
        P(),
        P(ROW, COL, None, None, None),
        P(ROW, COL, None),
        P(ROW, COL, None),
        P(ROW, COL),
        P(ROW + COL, None),
    )
    return jax.shard_map(
        shards,
        mesh=fine,
        in_specs=placed,
        out_specs=(P(ROW + COL, None), P(ROW + COL, None), P()),
        check_vma=False,
    )
```

```python
import functools

import jax
import jax.numpy as jnp
from jax import lax
from jax.experimental import pallas as pl
from jax.experimental.pallas import tpu as pltpu
from jax.sharding import Mesh, PartitionSpec as P

ROW = ("zb", "za", "xb", "xa")
Z = ("zb", "za")
GROUP = ("zb", "xb", "xa")
PLANE = ("x_lo", "y")
CORE = "core"
COL = PLANE + (CORE,)
UNROLL = 4
VMEM_LIMIT = 32 * 1024 * 1024

SMEM_SPEC = pl.BlockSpec(memory_space=pltpu.SMEM)
VMEM_SPEC = pl.BlockSpec(memory_space=pltpu.VMEM)


def row_place(block, core):
    return ((block & 1) ^ core) * 16 + (block >> 1)


def col_place(block, za):
    return (((block >> 2) & 1) ^ za) * 16 + ((block >> 3) * 4 + (block & 3))


def add_tiles(count, out_place, product, acc):
    spare = acc.shape[0] - 1

    def group(index, carry):
        first = index * UNROLL
        products = [product(first + j) for j in range(UNROLL)]
        for j in range(UNROLL):
            slot = first + j
            target = jnp.where(slot < count, out_place(slot), spare)
            acc[target] += products[j]
        return carry

    lax.fori_loop(0, (count + UNROLL - 1) // UNROLL, group, 0)


def forward_kernel(count_ref, rows_ref, cols_ref, tiles_ref, own_ref, low_ref, high_ref, keep_ref, send_ref, acc, stripe):
    core, za = lax.axis_index(CORE), lax.axis_index("za")
    half, part = own_ref.shape[0], low_ref.shape[0]
    stripe[:half] = own_ref[...]
    stripe[half : half + part] = low_ref[...]
    stripe[half + part :] = high_ref[...]
    acc[...] = jnp.zeros_like(acc)

    def product(k):
        features = stripe[col_place(cols_ref[0, k], za)]
        return jnp.dot(tiles_ref[k], features, preferred_element_type=jnp.float32)

    add_tiles(count_ref[0, 0], lambda k: row_place(rows_ref[0, k], core), product, acc)
    half = keep_ref.shape[0]
    keep_ref[...] = acc[:half]
    send_ref[...] = acc[half : 2 * half].astype(send_ref.dtype)


def dense_kernel(terms_ref, weight_ref, cot_ref, hidden_ref, payload_ref):
    groups, owned, _ = terms_ref.shape
    total = terms_ref[0].astype(jnp.float32)
    for i in range(1, groups):
        total += terms_ref[i].astype(jnp.float32)
    aggregated = total.astype(jnp.bfloat16)
    weight = weight_ref[...]
    preact = jnp.dot(aggregated, weight, preferred_element_type=jnp.float32)
    capped = jnp.minimum(preact, 0.0)
    grown = jnp.exp(capped)
    negative = grown - 1.0
    hidden_ref[...] = jnp.where(preact > 0, preact, negative).astype(jnp.bfloat16)
    slope = jnp.where(preact > 0, 1.0, grown)
    upstream = (cot_ref[...].astype(jnp.float32) * slope).astype(jnp.bfloat16)
    grad = lax.dot_general(
        aggregated, upstream, (((0,), (0,)), ((), ())), preferred_element_type=jnp.float32
    )
    back = lax.dot_general(
        weight, upstream, (((1,), (1,)), ((), ())), preferred_element_type=jnp.float32
    ).astype(jnp.bfloat16)
    step = grad.shape[0] // groups
    for i in range(groups):
        piece = grad[i * step : (i + 1) * step]
        packed = jnp.concatenate([piece[:, :128], piece[:, 128:]], axis=0)
        payload_ref[i, :owned] = back
        payload_ref[i, owned:] = packed.astype(jnp.bfloat16)


def backward_kernel(
    count_ref, rows_ref, cols_ref, tiles_ref, own_ref, other_ref, keep_ref, grad_ref, up_ref, down_ref, acc, stripe
):
    core, za = lax.axis_index(CORE), lax.axis_index("za")
    half = own_ref.shape[0]
    owned = stripe.shape[1]
    stripe[:half] = own_ref[:, :owned]
    stripe[half:] = other_ref[:, :owned]
    acc[...] = jnp.zeros_like(acc)

    def product(k):
        upstream = stripe[row_place(rows_ref[0, k], core)]
        return jnp.dot(upstream, tiles_ref[k], preferred_element_type=jnp.float32)

    add_tiles(count_ref[0, 0], lambda k: col_place(cols_ref[0, k], za), product, acc)
    grad = own_ref[0, owned:].astype(jnp.float32) + other_ref[0, owned:].astype(jnp.float32)
    for i in range(1, half):
        grad += own_ref[i, owned:].astype(jnp.float32) + other_ref[i, owned:].astype(jnp.float32)
    grad_ref[...] = grad
    half = keep_ref.shape[0]
    keep_ref[...] = acc[:half]
    for i in range(half // 2):
        up_ref[i * owned : (i + 1) * owned] = acc[half + i].astype(up_ref.dtype)
        down_ref[i * owned : (i + 1) * owned] = acc[half + half // 2 + i].astype(down_ref.dtype)
    up_ref[half // 2 * owned :] = grad.astype(up_ref.dtype)


def middle_kernel(keep_ref, grad_ref, low_ref, high_ref, out_ref):
    half, owned, _ = keep_ref.shape
    part = half // 2
    grad = (grad_ref[...] + low_ref[part * owned :].astype(jnp.float32)).astype(out_ref.dtype)
    for i in range(half):
        came = (low_ref if i < part else high_ref)[i % part * owned : (i % part + 1) * owned]
        out_ref[i, :owned] = (keep_ref[i] + came.astype(jnp.float32)).astype(out_ref.dtype)
        out_ref[i, owned:] = grad


def final_kernel(terms_ref, grad_x_ref, piece_ref):
    groups, rows, owned = terms_ref.shape
    total = terms_ref[0].astype(jnp.float32)
    for i in range(1, groups):
        total += terms_ref[i].astype(jnp.float32)
    grad_x_ref[...] = total[:owned].T.astype(grad_x_ref.dtype)
    step = (rows - owned) // 2
    piece = jnp.concatenate([total[owned : owned + step], total[owned + step :]], axis=1)
    for i in range(piece_ref.shape[0]):
        piece_ref[i] = piece


def call(kernel, name, outs, in_specs, scratch=()):
    return pl.pallas_call(
        kernel,
        name=name,
        out_shape=outs,
        in_specs=in_specs,
        out_specs=jax.tree.map(lambda _: VMEM_SPEC, outs),
        scratch_shapes=list(scratch),
        compiler_params=pltpu.CompilerParams(vmem_limit_bytes=VMEM_LIMIT),
    )


def shards(features, weight, tile_vals, tile_rows, tile_cols, tile_counts, cotangent):
    bf16, f32 = jnp.bfloat16, jnp.float32
    shape = jax.ShapeDtypeStruct
    tiles = tile_vals[0, 0]
    rows, cols = tile_rows[0], tile_cols[0]
    owned, width = features.shape
    hid = weight.shape[1]
    n_row, n_plane = lax.axis_size(ROW), lax.axis_size(PLANE)
    half, part = n_row // 2, n_row // 4
    extra = 2 * width // n_plane
    swap = [(0, 1), (1, 0)]
    n_z = lax.axis_size(Z)
    up = [(i, (i + 1) % n_z) for i in range(n_z)]
    down = [(i, (i - 1) % n_z) for i in range(n_z)]
    tile_specs = [SMEM_SPEC] * 3 + [VMEM_SPEC] * 3

    spread = jnp.broadcast_to(features[None], (half, owned, width))
    own = lax.all_to_all(spread, GROUP, 0, 0)
    low = lax.ppermute(own[:part], Z, up)
    high = lax.ppermute(own[part:], Z, down)
    keep, send = call(
        forward_kernel,
        "forward_tiles",
        (shape((n_plane, owned, width), f32), shape((n_plane, owned, width), bf16)),
        tile_specs + [VMEM_SPEC],
        [pltpu.VMEM((2 * n_plane + 1, owned, width), f32), pltpu.VMEM((n_row, owned, width), bf16)],
    )(tile_counts, rows, cols, tiles, own, low, high)
    terms = (keep + lax.ppermute(send, CORE, swap).astype(f32)).astype(bf16)
    terms = lax.all_to_all(terms, PLANE, 0, 0)
    hidden, payload = call(
        dense_kernel,
        "dense",
        (shape((owned, hid), bf16), shape((n_plane, owned + extra, width), bf16)),
        [VMEM_SPEC] * 3,
    )(terms, weight, cotangent)
    own = lax.all_to_all(payload, PLANE, 0, 0)
    other = lax.ppermute(own, CORE, swap)
    keep, grad, to_up, to_down = call(
        backward_kernel,
        "backward_tiles",
        (
            shape((half, width, owned), f32),
            shape((extra, width), f32),
            shape((part * width + extra, owned), bf16),
            shape((part * width, owned), bf16),
        ),
        tile_specs,
        [pltpu.VMEM((n_row + 1, width, owned), f32), pltpu.VMEM((2 * n_plane, width, owned), bf16)],
    )(tile_counts, rows, cols, tiles, own, other)
    low = lax.ppermute(to_up, Z, up)
    high = lax.ppermute(to_down, Z, down)
    back = call(middle_kernel, "middle", shape((half, width + extra, owned), bf16), [VMEM_SPEC] * 4)(
        keep, grad, low, high
    )
    back = lax.all_to_all(back, GROUP, 0, 0)
    grad_x, piece = call(
        final_kernel,
        "final",
        (shape((owned, width), bf16), shape((n_plane, width // n_plane, hid), f32)),
        [VMEM_SPEC],
    )(back)
    grad_w = lax.all_to_all(piece, PLANE, 0, 0).reshape(width, hid)
    return hidden, grad_x, grad_w


def solution(mesh):
    fine = Mesh(mesh.devices.reshape(4, 2, 2, 2, 2, 8, 2), ROW + COL)
    placed = (
        P(ROW + COL, None),
        P(),
        P(ROW, COL, None, None, None),
        P(ROW, COL, None),
        P(ROW, COL, None),
        P(ROW, COL),
        P(ROW + COL, None),
    )
    return jax.shard_map(
        shards,
        mesh=fine,
        in_specs=placed,
        out_specs=(P(ROW + COL, None), P(ROW + COL, None), P()),
        check_vma=False,
    )
```

```python
import functools

import jax
import jax.numpy as jnp
from jax import lax
from jax.experimental import pallas as pl
from jax.experimental.pallas import tpu as pltpu
from jax.sharding import Mesh, PartitionSpec as P

ROW = ("zb", "za", "xb", "xa")
Z = ("zb", "za")
GROUP = ("xb", "xa", "zb")
PLANE = ("x_lo", "y")
CORE = "core"
COL = PLANE + (CORE,)
UNROLL = 16
VMEM_LIMIT = 32 * 1024 * 1024

SMEM_SPEC = pl.BlockSpec(memory_space=pltpu.SMEM)
VMEM_SPEC = pl.BlockSpec(memory_space=pltpu.VMEM)


def row_place(block, core):
    return ((block & 1) ^ core) * 16 + (block >> 1)


def col_place(block, za):
    return (((block >> 2) & 1) ^ za) * 16 + ((block & 3) * 4 + (block >> 3))


def add_tiles(count, out_place, product, acc):
    spare = acc.shape[0] - 1

    def group(index, carry):
        first = index * UNROLL
        products = [product(first + j) for j in range(UNROLL)]
        for j in range(UNROLL):
            slot = first + j
            target = jnp.where(slot < count, out_place(slot), spare)
            acc[target] += products[j]
        return carry

    lax.fori_loop(0, (count + UNROLL - 1) // UNROLL, group, 0)


def forward_kernel(count_ref, rows_ref, cols_ref, tiles_ref, own_ref, low_ref, high_ref, keep_ref, send_ref, acc, stripe):
    core, za = lax.axis_index(CORE), lax.axis_index("za")
    half, part = own_ref.shape[0], low_ref.shape[0]
    stripe[:half] = own_ref[...]
    stripe[half : half + part] = low_ref[...]
    stripe[half + part :] = high_ref[...]
    acc[...] = jnp.zeros_like(acc)

    def product(k):
        features = stripe[col_place(cols_ref[0, k], za)]
        return jnp.dot(tiles_ref[k], features, preferred_element_type=jnp.float32)

    add_tiles(count_ref[0, 0], lambda k: row_place(rows_ref[0, k], core), product, acc)
    half = keep_ref.shape[0]
    keep_ref[...] = acc[:half]
    send_ref[...] = acc[half : 2 * half].astype(send_ref.dtype)


def dense_kernel(terms_ref, weight_ref, cot_ref, hidden_ref, payload_ref):
    groups, owned, _ = terms_ref.shape
    total = terms_ref[0].astype(jnp.float32)
    for i in range(1, groups):
        total += terms_ref[i].astype(jnp.float32)
    aggregated = total.astype(jnp.bfloat16)
    weight = weight_ref[...]
    preact = jnp.dot(aggregated, weight, preferred_element_type=jnp.float32)
    capped = jnp.minimum(preact, 0.0)
    grown = jnp.exp(capped)
    negative = grown - 1.0
    hidden_ref[...] = jnp.where(preact > 0, preact, negative).astype(jnp.bfloat16)
    slope = jnp.where(preact > 0, 1.0, grown)
    upstream = (cot_ref[...].astype(jnp.float32) * slope).astype(jnp.bfloat16)
    grad = lax.dot_general(
        aggregated, upstream, (((0,), (0,)), ((), ())), preferred_element_type=jnp.float32
    )
    back = lax.dot_general(
        weight, upstream, (((1,), (1,)), ((), ())), preferred_element_type=jnp.float32
    ).astype(jnp.bfloat16)
    step = grad.shape[0] // groups
    for i in range(groups):
        piece = grad[i * step : (i + 1) * step]
        packed = jnp.concatenate([piece[:, :128], piece[:, 128:]], axis=0)
        payload_ref[i, :owned] = back
        payload_ref[i, owned:] = packed.astype(jnp.bfloat16)


def backward_kernel(
    count_ref, rows_ref, cols_ref, tiles_ref, own_ref, other_ref, keep_ref, grad_ref, up_ref, down_ref, acc, stripe
):
    core, za = lax.axis_index(CORE), lax.axis_index("za")
    half = own_ref.shape[0]
    owned = stripe.shape[1]
    stripe[:half] = own_ref[:, :owned]
    stripe[half:] = other_ref[:, :owned]
    acc[...] = jnp.zeros_like(acc)

    def product(k):
        upstream = stripe[row_place(rows_ref[0, k], core)]
        return jnp.dot(upstream, tiles_ref[k], preferred_element_type=jnp.float32)

    add_tiles(count_ref[0, 0], lambda k: col_place(cols_ref[0, k], za), product, acc)
    grad = own_ref[0, owned:].astype(jnp.float32) + other_ref[0, owned:].astype(jnp.float32)
    for i in range(1, half):
        grad += own_ref[i, owned:].astype(jnp.float32) + other_ref[i, owned:].astype(jnp.float32)
    grad_ref[...] = grad
    half = keep_ref.shape[0]
    keep_ref[...] = acc[:half]
    for i in range(half // 2):
        up_ref[i * owned : (i + 1) * owned] = acc[half + i].astype(up_ref.dtype)
        down_ref[i * owned : (i + 1) * owned] = acc[half + half // 2 + i].astype(down_ref.dtype)
    up_ref[half // 2 * owned :] = grad.astype(up_ref.dtype)


def middle_kernel(keep_ref, grad_ref, low_ref, high_ref, out_ref):
    half, owned, _ = keep_ref.shape
    part = half // 2
    grad = (grad_ref[...] + low_ref[part * owned :].astype(jnp.float32)).astype(out_ref.dtype)
    for i in range(half):
        came = (low_ref if i < part else high_ref)[i % part * owned : (i % part + 1) * owned]
        out_ref[i, :owned] = (keep_ref[i] + came.astype(jnp.float32)).astype(out_ref.dtype)
        out_ref[i, owned:] = grad


def final_kernel(terms_ref, grad_x_ref, piece_ref):
    groups, rows, owned = terms_ref.shape
    total = terms_ref[0].astype(jnp.float32)
    for i in range(1, groups):
        total += terms_ref[i].astype(jnp.float32)
    grad_x_ref[...] = total[:owned].T.astype(grad_x_ref.dtype)
    step = (rows - owned) // 2
    piece = jnp.concatenate([total[owned : owned + step], total[owned + step :]], axis=1)
    for i in range(piece_ref.shape[0]):
        piece_ref[i] = piece


def call(kernel, name, outs, in_specs, scratch=()):
    return pl.pallas_call(
        kernel,
        name=name,
        out_shape=outs,
        in_specs=in_specs,
        out_specs=jax.tree.map(lambda _: VMEM_SPEC, outs),
        scratch_shapes=list(scratch),
        compiler_params=pltpu.CompilerParams(vmem_limit_bytes=VMEM_LIMIT),
    )


def shards(features, weight, tile_vals, tile_rows, tile_cols, tile_counts, cotangent):
    bf16, f32 = jnp.bfloat16, jnp.float32
    shape = jax.ShapeDtypeStruct
    tiles = tile_vals[0, 0]
    rows, cols = tile_rows[0], tile_cols[0]
    owned, width = features.shape
    hid = weight.shape[1]
    n_row, n_plane = lax.axis_size(ROW), lax.axis_size(PLANE)
    half, part = n_row // 2, n_row // 4
    extra = 2 * width // n_plane
    swap = [(0, 1), (1, 0)]
    n_z = lax.axis_size(Z)
    up = [(i, (i + 1) % n_z) for i in range(n_z)]
    down = [(i, (i - 1) % n_z) for i in range(n_z)]
    tile_specs = [SMEM_SPEC] * 3 + [VMEM_SPEC] * 3

    spread = jnp.broadcast_to(features[None], (half, owned, width))
    own = lax.all_to_all(spread, GROUP, 0, 0)
    low = lax.ppermute(own[:part], Z, up)
    high = lax.ppermute(own[part:], Z, down)
    keep, send = call(
        forward_kernel,
        "forward_tiles",
        (shape((n_plane, owned, width), f32), shape((n_plane, owned, width), bf16)),
        tile_specs + [VMEM_SPEC],
        [pltpu.VMEM((2 * n_plane + 1, owned, width), f32), pltpu.VMEM((n_row, owned, width), bf16)],
    )(tile_counts, rows, cols, tiles, own, low, high)
    terms = (keep + lax.ppermute(send, CORE, swap).astype(f32)).astype(bf16)
    terms = lax.all_to_all(terms, PLANE, 0, 0)
    hidden, payload = call(
        dense_kernel,
        "dense",
        (shape((owned, hid), bf16), shape((n_plane, owned + extra, width), bf16)),
        [VMEM_SPEC] * 3,
    )(terms, weight, cotangent)
    own = lax.all_to_all(payload, PLANE, 0, 0)
    other = lax.ppermute(own, CORE, swap)
    keep, grad, to_up, to_down = call(
        backward_kernel,
        "backward_tiles",
        (
            shape((half, width, owned), f32),
            shape((extra, width), f32),
            shape((part * width + extra, owned), bf16),
            shape((part * width, owned), bf16),
        ),
        tile_specs,
        [pltpu.VMEM((n_row + 1, width, owned), f32), pltpu.VMEM((2 * n_plane, width, owned), bf16)],
    )(tile_counts, rows, cols, tiles, own, other)
    low = lax.ppermute(to_up, Z, up)
    high = lax.ppermute(to_down, Z, down)
    back = call(middle_kernel, "middle", shape((half, width + extra, owned), bf16), [VMEM_SPEC] * 4)(
        keep, grad, low, high
    )
    back = lax.all_to_all(back, GROUP, 0, 0)
    grad_x, piece = call(
        final_kernel,
        "final",
        (shape((owned, width), bf16), shape((n_plane, width // n_plane, hid), f32)),
        [VMEM_SPEC],
    )(back)
    grad_w = lax.all_to_all(piece, PLANE, 0, 0).reshape(width, hid)
    return hidden, grad_x, grad_w


def solution(mesh):
    fine = Mesh(mesh.devices.reshape(4, 2, 2, 2, 2, 8, 2), ROW + COL)
    placed = (
        P(ROW + COL, None),
        P(),
        P(ROW, COL, None, None, None),
        P(ROW, COL, None),
        P(ROW, COL, None),
        P(ROW, COL),
        P(ROW + COL, None),
    )
    return jax.shard_map(
        shards,
        mesh=fine,
        in_specs=placed,
        out_specs=(P(ROW + COL, None), P(ROW + COL, None), P()),
        check_vma=False,
    )
```

```python
import functools

import jax
import jax.numpy as jnp
from jax import lax
from jax.experimental import pallas as pl
from jax.experimental.pallas import tpu as pltpu
from jax.sharding import Mesh, PartitionSpec as P

ROW = ("zb", "za", "xb", "xa")
Z = ("zb", "za")
GROUP = ("xb", "xa", "zb")
PLANE = ("x_lo", "y")
CORE = "core"
COL = PLANE + (CORE,)
UNROLL = 16
VMEM_LIMIT = 32 * 1024 * 1024

SMEM_SPEC = pl.BlockSpec(memory_space=pltpu.SMEM)
VMEM_SPEC = pl.BlockSpec(memory_space=pltpu.VMEM)


def row_place(block, core):
    return ((block & 1) ^ core) * 16 + (block >> 1)


def col_place(block, za):
    return (((block >> 2) & 1) ^ za) * 16 + ((block & 3) * 4 + (block >> 3))


def add_tiles(count, out_place, product, acc):
    spare = acc.shape[0] - 1

    def group(index, carry):
        first = index * UNROLL
        products = [product(first + j) for j in range(UNROLL)]
        for j in range(UNROLL):
            slot = first + j
            target = jnp.where(slot < count, out_place(slot), spare)
            acc[target] += products[j]
        return carry

    lax.fori_loop(0, (count + UNROLL - 1) // UNROLL, group, 0)


def forward_kernel(count_ref, rows_ref, cols_ref, tiles_ref, own_ref, low_ref, high_ref, keep_ref, send_ref, acc, stripe):
    core, za = lax.axis_index(CORE), lax.axis_index("za")
    half, part = own_ref.shape[0], low_ref.shape[0]
    stripe[:half] = own_ref[...]
    stripe[half : half + part] = low_ref[...]
    stripe[half + part :] = high_ref[...]
    acc[...] = jnp.zeros_like(acc)

    def product(k):
        features = stripe[col_place(cols_ref[0, k], za)]
        return jnp.dot(tiles_ref[k], features, preferred_element_type=jnp.float32)

    add_tiles(count_ref[0, 0], lambda k: row_place(rows_ref[0, k], core), product, acc)
    half = keep_ref.shape[0]
    keep_ref[...] = acc[:half]
    send_ref[...] = acc[half : 2 * half].astype(send_ref.dtype)


def dense_kernel(terms_ref, weight_ref, cot_ref, hidden_ref, payload_ref):
    groups, owned, _ = terms_ref.shape
    total = terms_ref[0].astype(jnp.float32)
    for i in range(1, groups):
        total += terms_ref[i].astype(jnp.float32)
    aggregated = total.astype(jnp.bfloat16)
    weight = weight_ref[...]
    preact = jnp.dot(aggregated, weight, preferred_element_type=jnp.float32)
    capped = jnp.minimum(preact, 0.0)
    grown = jnp.exp(capped)
    negative = grown - 1.0
    hidden_ref[...] = jnp.where(preact > 0, preact, negative).astype(jnp.bfloat16)
    slope = jnp.where(preact > 0, 1.0, grown)
    upstream = (cot_ref[...].astype(jnp.float32) * slope).astype(jnp.bfloat16)
    grad = lax.dot_general(
        aggregated, upstream, (((0,), (0,)), ((), ())), preferred_element_type=jnp.float32
    )
    back = lax.dot_general(
        weight, upstream, (((1,), (1,)), ((), ())), preferred_element_type=jnp.float32
    ).astype(jnp.bfloat16)
    step = grad.shape[0] // groups
    for i in range(groups):
        piece = grad[i * step : (i + 1) * step]
        packed = jnp.concatenate([piece[:, :128], piece[:, 128:]], axis=0)
        payload_ref[i, :owned] = back
        payload_ref[i, owned:] = packed.astype(jnp.bfloat16)


def backward_kernel(
    count_ref, rows_ref, cols_ref, tiles_ref, own_ref, other_ref, keep_ref, grad_ref, send_ref, acc, stripe
):
    core, za = lax.axis_index(CORE), lax.axis_index("za")
    half = own_ref.shape[0]
    owned = stripe.shape[1]
    stripe[:half] = own_ref[:, :owned]
    stripe[half:] = other_ref[:, :owned]
    acc[...] = jnp.zeros_like(acc)

    def product(k):
        upstream = stripe[row_place(rows_ref[0, k], core)]
        return jnp.dot(upstream, tiles_ref[k], preferred_element_type=jnp.float32)

    add_tiles(count_ref[0, 0], lambda k: col_place(cols_ref[0, k], za), product, acc)
    grad = own_ref[0, owned:].astype(jnp.float32) + other_ref[0, owned:].astype(jnp.float32)
    for i in range(1, half):
        grad += own_ref[i, owned:].astype(jnp.float32) + other_ref[i, owned:].astype(jnp.float32)
    grad_ref[...] = grad
    half = keep_ref.shape[0]
    keep_ref[...] = acc[:half]
    for i in range(half):
        send_ref[i * owned : (i + 1) * owned] = acc[half + i].astype(send_ref.dtype)
    send_ref[half * owned :] = grad.astype(send_ref.dtype)


def middle_kernel(keep_ref, grad_ref, came_ref, out_ref):
    half, owned, _ = keep_ref.shape
    grad = (grad_ref[...] + came_ref[half * owned :].astype(jnp.float32)).astype(out_ref.dtype)
    for i in range(half):
        came = came_ref[i * owned : (i + 1) * owned]
        out_ref[i, :owned] = (keep_ref[i] + came.astype(jnp.float32)).astype(out_ref.dtype)
        out_ref[i, owned:] = grad


def final_kernel(terms_ref, grad_x_ref, piece_ref):
    groups, rows, owned = terms_ref.shape
    total = terms_ref[0].astype(jnp.float32)
    for i in range(1, groups):
        total += terms_ref[i].astype(jnp.float32)
    grad_x_ref[...] = total[:owned].T.astype(grad_x_ref.dtype)
    step = (rows - owned) // 2
    piece = jnp.concatenate([total[owned : owned + step], total[owned + step :]], axis=1)
    for i in range(piece_ref.shape[0]):
        piece_ref[i] = piece


def call(kernel, name, outs, in_specs, scratch=()):
    return pl.pallas_call(
        kernel,
        name=name,
        out_shape=outs,
        in_specs=in_specs,
        out_specs=jax.tree.map(lambda _: VMEM_SPEC, outs),
        scratch_shapes=list(scratch),
        compiler_params=pltpu.CompilerParams(vmem_limit_bytes=VMEM_LIMIT),
    )


def shards(features, weight, tile_vals, tile_rows, tile_cols, tile_counts, cotangent):
    bf16, f32 = jnp.bfloat16, jnp.float32
    shape = jax.ShapeDtypeStruct
    tiles = tile_vals[0, 0]
    rows, cols = tile_rows[0], tile_cols[0]
    owned, width = features.shape
    hid = weight.shape[1]
    n_row, n_plane = lax.axis_size(ROW), lax.axis_size(PLANE)
    half, part = n_row // 2, n_row // 4
    extra = 2 * width // n_plane
    swap = [(0, 1), (1, 0)]
    n_z = lax.axis_size(Z)
    up = [(i, (i + 1) % n_z) for i in range(n_z)]
    down = [(i, (i - 1) % n_z) for i in range(n_z)]
    tile_specs = [SMEM_SPEC] * 3 + [VMEM_SPEC] * 3

    spread = jnp.broadcast_to(features[None], (half, owned, width))
    own = lax.all_to_all(spread, GROUP, 0, 0)
    low = lax.ppermute(own[:part], Z, up)
    high = lax.ppermute(own[part:], Z, down)
    keep, send = call(
        forward_kernel,
        "forward_tiles",
        (shape((n_plane, owned, width), f32), shape((n_plane, owned, width), bf16)),
        tile_specs + [VMEM_SPEC],
        [pltpu.VMEM((2 * n_plane + 1, owned, width), f32), pltpu.VMEM((n_row, owned, width), bf16)],
    )(tile_counts, rows, cols, tiles, own, low, high)
    terms = (keep + lax.ppermute(send, CORE, swap).astype(f32)).astype(bf16)
    terms = lax.all_to_all(terms, PLANE, 0, 0)
    hidden, payload = call(
        dense_kernel,
        "dense",
        (shape((owned, hid), bf16), shape((n_plane, owned + extra, width), bf16)),
        [VMEM_SPEC] * 3,
    )(terms, weight, cotangent)
    own = lax.all_to_all(payload, PLANE, 0, 0)
    other = lax.ppermute(own, CORE, swap)
    keep, grad, send = call(
        backward_kernel,
        "backward_tiles",
        (
            shape((half, width, owned), f32),
            shape((extra, width), f32),
            shape((half * width + extra, owned), bf16),
        ),
        tile_specs,
        [pltpu.VMEM((n_row + 1, width, owned), f32), pltpu.VMEM((2 * n_plane, width, owned), bf16)],
    )(tile_counts, rows, cols, tiles, own, other)
    came = lax.ppermute(send, "za", swap)
    back = call(middle_kernel, "middle", shape((half, width + extra, owned), bf16), [VMEM_SPEC] * 3)(
        keep, grad, came
    )
    back = lax.all_to_all(back, GROUP, 0, 0)
    grad_x, piece = call(
        final_kernel,
        "final",
        (shape((owned, width), bf16), shape((n_plane, width // n_plane, hid), f32)),
        [VMEM_SPEC],
    )(back)
    grad_w = lax.all_to_all(piece, PLANE, 0, 0).reshape(width, hid)
    return hidden, grad_x, grad_w


def solution(mesh):
    fine = Mesh(mesh.devices.reshape(4, 2, 2, 2, 2, 8, 2), ROW + COL)
    placed = (
        P(ROW + COL, None),
        P(),
        P(ROW, COL, None, None, None),
        P(ROW, COL, None),
        P(ROW, COL, None),
        P(ROW, COL),
        P(ROW + COL, None),
    )
    return jax.shard_map(
        shards,
        mesh=fine,
        in_specs=placed,
        out_specs=(P(ROW + COL, None), P(ROW + COL, None), P()),
        check_vma=False,
    )
```
